1024 devices in a mesh: dp: 32 (over y, x, core), expert: 32 (over z).
Axes of the slice: x: 4, y: 4, z: 32, core: 2. Of those that a mesh axis runs over, the one named last changes fastest.
Arguments:
- token_values: bfloat16 [131072, 2560], P(('dp', 'expert')), may hold values from -6 to 6
- token_scales: float32 [131072, 20], P(('dp', 'expert')), may hold values from 0.25 to 4
- out_grad: bfloat16 [131072, 2560], P(('dp', 'expert')), may hold values from -6 to 6
- route_expert: int32 [131072, 1], P(('dp', 'expert')), may hold values from 0 to 31; in each aligned block of 128 rows (0 to 127, 128 to 255, ...) at most 5 rows name the same one
- gate: bfloat16 [131072, 1], P(('dp', 'expert')), may hold values from 0.049804688 to 1
- up_weight: bfloat16 [32, 2560, 768], P('expert'), may hold values from -0.125 to 0.125
- down_weight: bfloat16 [32, 768, 2560], P('expert'), may hold values from -0.21875 to 0.21875
Outputs:
- token_grad: bfloat16 [131072, 2560], P(('dp', 'expert'))
- gate_grad: bfloat16 [131072, 1], P(('dp', 'expert'))
- down_grad: float32 [32, 768, 2560], P('expert', 'dp')
The draws below stay inside these ranges and needn't reach their ends.
Inputs may be any that keep to these rules, and one draw needn't show every extreme that they name: `route_expert`: among the rows of one device no expert is named by more than 5 routes; on some device one expert is named by exactly 5.
All inputs are finite; a program needn't handle non-finite values.
Results may differ from the reference program's by a relative error of at most 0.018.
Values may be sent and summed in bfloat16 or wider, within the bound.
A program may use at most 64 MiB of HBM per device.

```python
import math
import jax
import jax.numpy as jnp
import numpy as np
from jax import lax

D = 2560
H = 768
TOP = 1
TOK_DEV = 128
EXPERTS = 32
CAP = 5
TOKENS = 131072
N_DP = 32
N_EXPERT = 32


def block_levels(stream_key, shape, pieces, least, high):
    def one(position, shards_of):
        heights = jax.random.uniform(jax.random.fold_in(jax.random.fold_in(stream_key, 6), position), (shards_of,), jnp.float32, least / len(pieces), high / len(pieces))
        return jnp.repeat(jnp.exp(heights), shape[position] // shards_of).reshape((-1,) + (1,) * (len(shape) - position - 1))

    factor_of = one(*pieces[0])
    for cut in pieces[1:]:
        factor_of = factor_of * one(*cut)
    return factor_of


def deal_out(rng, own, number, rows, number_of, top, limit, lean):
    order = jax.random.permutation(rng, number_of)
    packed, ordinary = shares(number_of, rows * top, limit, lean, True), shares(number_of, rows * top, limit, lean, False)
    places = jnp.arange(number_of)

    def named(tallies, rotation):
        used = int((tallies > 0).sum())
        fixed = max(1, used // 4)
        passed = fixed + (places - fixed + rotation * (used - fixed)) % max(1, number_of - fixed)
        return jnp.zeros((number_of,), jnp.int32).at[order[jnp.where(places < fixed, places, passed)]].set(jnp.asarray(tallies, jnp.int32))

    tallies = jnp.where(number % 4 == 0, named(packed, number // 4), named(ordinary, number - number // 4 - 1))
    mixed = jax.random.permutation(jax.random.fold_in(own, 3), number_of)
    source_of, receiver = mixed[0:number_of // 2 * 2:2], mixed[1:number_of // 2 * 2:2]
    room = jnp.minimum(tallies[source_of] - 1, limit - tallies[receiver]) // 2
    room = jnp.where((source_of == order[0]) | (receiver == order[0]) | (tallies[receiver] == 0), 0, jnp.maximum(room, 0))
    passed = jax.random.randint(jax.random.fold_in(own, 4), (number_of // 2,), 0, 1 << 20) % (room + 1)
    tallies = tallies.at[source_of].add(-passed).at[receiver].add(passed)
    members = jnp.searchsorted(jnp.cumsum(tallies), jnp.arange(rows * top), side="right").astype(jnp.int32)
    grid = members.reshape(top, rows).T
    grid = grid[jax.random.permutation(jax.random.fold_in(own, 1), rows)]
    rotation = jax.random.randint(jax.random.fold_in(own, 2), (rows, 1), 0, top)
    return jnp.take_along_axis(grid, (jnp.arange(top)[None, :] + rotation) % top, axis=1)


def shares(amount, total, reach, skew, full):
    loads = [(1 << 20) // math.isqrt(grade ** skew) + 1 for grade in range(1, amount + 1)]
    largest = reach if full else min(reach, max(-(-total // amount), total * loads[0] // sum(loads)))
    least = 1 if total - largest >= amount - 1 else 0
    given, surplus = [largest] + [least] * (amount - 1), total - largest - least * (amount - 1)
    while surplus > 0:
        candidates = [i for i in range(1, amount) if given[i] < largest] or [i for i in range(1, amount) if given[i] < reach]
        pool, remaining = sum([loads[i] for i in candidates]), surplus
        for i in candidates:
            more = min(reach - given[i], max(1, remaining * loads[i] // pool), surplus)
            given[i] = given[i] + more
            surplus = surplus - more
    return np.array(given)


def scatter_about(own_key, dims, scale, most, pieces=(), held_as=jnp.bfloat16):
    loudness = block_levels(own_key, dims, pieces, -0.22, 0.18) if pieces else 1.0
    values = jax.random.normal(own_key, dims, jnp.float32) * scale * loudness
    return jnp.minimum(jnp.maximum(values, -most), most).astype(held_as)


def setup_inputs(seed: int = 0) -> dict:
    key_list = jax.random.split(jax.random.key(seed), 8)
    token_values = scatter_about(key_list[0], (TOKENS, D), 1.0, 6.0, ((0, 1024),))
    token_scales = jnp.clip(jnp.exp(math.log(4.0) - 2.7725887 * jax.random.uniform(key_list[1], (TOKENS, D // 128), jnp.float32) ** block_levels(key_list[1], (TOKENS, D // 128), ((0, 1024),), -0.2, 0.2)), 0.25, 4.0)
    out_grad = scatter_about(key_list[2], (TOKENS, D), 1.0, 6.0, ((0, 1024),))
    route_expert_keys = jax.random.split(jax.random.fold_in(key_list[3], 1), TOKENS // TOK_DEV)
    route_expert_turns = jax.random.permutation(jax.random.fold_in(key_list[3], 3), TOKENS // TOK_DEV)
    route_expert = jax.vmap(lambda own, number: deal_out(jax.random.fold_in(key_list[3], 2), own, number, TOK_DEV, EXPERTS, TOP, CAP, 2))(route_expert_keys, route_expert_turns).reshape((TOKENS, TOP))
    gate = jnp.clip(jnp.exp(math.log(1.0) - 2.9996462 * jax.random.uniform(key_list[4], (TOKENS, TOP), jnp.float32) ** block_levels(key_list[4], (TOKENS, TOP), ((0, 1024),), -0.2, 0.2)), 0.049804688, 1.0).astype(jnp.bfloat16)
    up_weight = scatter_about(key_list[5], (EXPERTS, D, H), D ** -0.5, 0.125, ((0, 32),))
    down_weight = scatter_about(key_list[6], (EXPERTS, H, D), H ** -0.5, 0.21875, ((0, 32),))
    return {"token_values": token_values, "token_scales": token_scales, "out_grad": out_grad, "route_expert": route_expert, "gate": gate, "up_weight": up_weight, "down_weight": down_weight}


def dequantize(values, scales):
    count, width = values.shape
    blocks = scales.shape[1]
    wide = values.astype(jnp.float32).reshape(count, blocks, width // blocks) * scales[:, :, None]
    return wide.reshape(count, width).astype(jnp.bfloat16)


def place_slots(route_ids, experts, capacity):
    flat = route_ids.reshape(-1).astype(jnp.int32)
    onehot = (flat[:, None] == jnp.arange(experts, dtype=jnp.int32)[None, :]).astype(jnp.int32)
    before = jnp.cumsum(onehot, axis=0) - onehot
    rank = jnp.sum(before * onehot, axis=1)
    return (flat * capacity + rank).astype(jnp.int32)


def expert_pass(inputs, grads, gates, up_w, down_w):
    pre = jnp.dot(inputs, up_w, preferred_element_type=jnp.float32)
    hidden = jax.nn.silu(pre).astype(jnp.bfloat16)
    back = lax.dot_general(grads, down_w, (((1,), (1,)), ((), ())), preferred_element_type=jnp.float32)
    gate_col = gates.astype(jnp.float32)[:, None]
    gate_term = jnp.sum(hidden.astype(jnp.float32) * back, axis=1).astype(jnp.bfloat16)
    sig = jax.nn.sigmoid(pre)
    pre_grad = (gate_col * back * sig * (1.0 + pre * (1.0 - sig))).astype(jnp.bfloat16)
    row_grad = lax.dot_general(pre_grad, up_w, (((1,), (1,)), ((), ())), preferred_element_type=jnp.float32).astype(jnp.bfloat16)
    scaled = (gate_col * grads.astype(jnp.float32)).astype(jnp.bfloat16)
    return row_grad, gate_term, hidden, scaled


def outer_sum(hidden, scaled):
    return lax.dot_general(hidden, scaled, (((0,), (0,)), ((), ())), preferred_element_type=jnp.float32)


def reference(token_values, token_scales, out_grad, route_expert, gate, up_weight, down_weight):
    width = token_values.shape[1]

    def split(arr):
        return arr.reshape((N_DP, N_EXPERT, TOK_DEV) + arr.shape[1:])

    def pack(values, scales, grads, ids, gates):
        inputs = dequantize(values, scales)
        slots = place_slots(ids, N_EXPERT, CAP)
        x_rows = jnp.repeat(inputs, TOP, axis=0)
        g_rows = jnp.repeat(grads, TOP, axis=0)
        x_buf = jnp.zeros((N_EXPERT * CAP, width), jnp.bfloat16).at[slots].set(x_rows)
        g_buf = jnp.zeros((N_EXPERT * CAP, width), jnp.bfloat16).at[slots].set(g_rows)
        w_buf = jnp.zeros((N_EXPERT * CAP,), jnp.bfloat16).at[slots].set(gates.reshape(-1))
        return x_buf.reshape(N_EXPERT, CAP, width), g_buf.reshape(N_EXPERT, CAP, width), w_buf.reshape(N_EXPERT, CAP)

    def unpack(row_buf, gate_buf, ids):
        slots = place_slots(ids, N_EXPERT, CAP)
        rows = row_buf.reshape(N_EXPERT * CAP, width)[slots]
        summed = jnp.sum(rows.reshape(TOK_DEV, TOP, width).astype(jnp.float32), axis=1).astype(jnp.bfloat16)
        return summed, gate_buf.reshape(N_EXPERT * CAP)[slots].reshape(TOK_DEV, TOP)

    def group_step(total, group):
        values, scales, grads, ids, gates = group
        x_buf, g_buf, w_buf = jax.vmap(pack)(values, scales, grads, ids, gates)
        x_exp = jnp.swapaxes(x_buf, 0, 1).reshape(N_EXPERT, N_EXPERT * CAP, width)
        g_exp = jnp.swapaxes(g_buf, 0, 1).reshape(N_EXPERT, N_EXPERT * CAP, width)
        w_exp = jnp.swapaxes(w_buf, 0, 1).reshape(N_EXPERT, N_EXPERT * CAP)

        def per_expert(args):
            inputs, grads_e, gates_e, up_w, down_w = args
            row_grad, gate_term, hidden, scaled = expert_pass(inputs, grads_e, gates_e, up_w, down_w)
            part = lax.optimization_barrier(outer_sum(hidden, scaled).astype(jnp.bfloat16))
            return row_grad, gate_term, part

        row_grad, gate_term, parts = lax.map(per_expert, (x_exp, g_exp, w_exp, up_weight, down_weight))
        total = total + parts.astype(jnp.float32)
        row_back = jnp.swapaxes(row_grad.reshape(N_EXPERT, N_EXPERT, CAP, width), 0, 1)
        gate_back = jnp.swapaxes(gate_term.reshape(N_EXPERT, N_EXPERT, CAP), 0, 1)
        token_part, gate_part = jax.vmap(unpack)(row_back, gate_back, ids)
        return total, (token_part, gate_part)

    start = jnp.zeros((N_EXPERT, H, width), jnp.float32)
    total, (token_grad, gate_grad) = lax.scan(group_step, start, (split(token_values), split(token_scales), split(out_grad), split(route_expert), split(gate)))
    return token_grad.reshape(TOKENS, width), gate_grad.reshape(TOKENS, TOP), total
```

```python
import jax
import jax.numpy as jnp
from jax import lax
from jax.experimental import pallas as pl
from jax.experimental.pallas import tpu as pltpu
from jax.sharding import PartitionSpec as P

MESH = pl.DeviceIdType.MESH
BF = jnp.bfloat16
F32 = jnp.float32
I32 = jnp.int32

N = 32
TOK = 128
D = 2560
H = 768
CAP = 5
LANE = 128
CHUNKS = D // LANE
TILE = 16
FWD_TILES = 13
RET_TILES = 7
FIRST = (0, 3, 6, 9, 12)
SUB = 8
BATCHES = N // SUB
RB = 64
HALF = D // 2
OUT_ROWS = H // N


def offset_of(k):
    half = (k + 1) // 2
    return jnp.where(k % 2 == 1, 16 - half, 16 + half)


def first_group(tile):
    return 16 * (tile // 5) + FIRST[tile % 5]


def tile_key(owner, rank, tau, g):
    place = rank + (CAP * (FIRST[tau] + g) - TILE * tau)
    good = (place >= 0) & (place < TILE)
    return jnp.where(good, owner * TILE + place, -1)


def ones_where(mask):
    return jnp.where(mask, 1.0, 0.0).astype(BF)


def kernel(
    values_ref, scales_ref, grad_ref, route_ref, gate_ref, up_hbm, down_hbm,
    token_ref, gate_out_ref, down_ref,
    up_ref, dn_ref, stack, send, recv, ret, back, part, part_in, pack_m, pick_m, unpack_m, repack_m,
    xs, hid, sc,
    w_sem, fs_sem, fr_sem, bs_sem, br_sem, ps_sem, pr_sem,
):
    dp = lax.axis_index("dp")
    ex = lax.axis_index("expert")

    up_copy = pltpu.make_async_copy(up_hbm.at[0], up_ref, w_sem.at[0])
    down_copy = pltpu.make_async_copy(down_hbm.at[0], dn_ref, w_sem.at[1])
    up_copy.start()
    down_copy.start()

    barrier = pltpu.get_barrier_semaphore()

    @pl.loop(1, N)
    def _(s):
        pl.semaphore_signal(
            barrier, inc=1, device_id=(dp, lax.rem(ex + s, N)), device_id_type=MESH
        )
        pl.semaphore_signal(
            barrier, inc=1, device_id=(lax.rem(dp + s, N), ex), device_id_type=MESH
        )

    r_col = route_ref[...].astype(F32)
    wide = jnp.broadcast_to(r_col, (TOK, TOK))
    tall = wide.T
    rows_i = lax.broadcasted_iota(I32, (TOK, TOK), 0)
    cols_i = lax.broadcasted_iota(I32, (TOK, TOK), 1)
    same = wide == tall
    rank_row = jnp.sum(jnp.where(same & (rows_i < cols_i), 1.0, 0.0), axis=0, keepdims=True).astype(I32)
    rank_col = jnp.sum(jnp.where(same & (cols_i < rows_i), 1.0, 0.0), axis=1, keepdims=True).astype(I32)
    r_row = tall[0:1, :].astype(I32)
    r_col = route_ref[...]

    gate = gate_ref[...].astype(F32)
    for c in range(CHUNKS):
        cols = slice(c * LANE, (c + 1) * LANE)
        stack[c * TOK : (c + 1) * TOK, :] = (
            values_ref[:, cols].astype(F32) * scales_ref[:, c : c + 1]
        ).astype(BF)
        stack[(CHUNKS + c) * TOK : (CHUNKS + c + 1) * TOK, :] = (
            gate * grad_ref[:, cols].astype(F32)
        ).astype(BF)
    stack[2 * CHUNKS * TOK :, :] = jnp.zeros((2 * TOK, LANE), BF)

    big = N * TILE
    row_id = lax.broadcasted_iota(I32, (big, TOK), 0)
    lane_id = lax.broadcasted_iota(I32, (TOK, big), 1)
    for tau in range(5):
        for g in range(4):
            key = tile_key(r_row, rank_row, tau, g)
            pack_m[tau, :, g * TOK : (g + 1) * TOK] = ones_where(row_id == key)
    for t in range(FWD_TILES):
        first = first_group(t)
        got = jnp.dot(
            pack_m[t % 5], stack[first * TOK : (first + 4) * TOK, :], preferred_element_type=F32
        )
        send[:, t * TILE : (t + 1) * TILE, :] = got.astype(BF).reshape(N, TILE, LANE)

    pl.semaphore_wait(barrier, 2 * (N - 1))

    def forward(k):
        to = lax.rem(ex + offset_of(k), N)
        return pltpu.make_async_remote_copy(
            src_ref=send.at[to],
            dst_ref=recv.at[k],
            send_sem=fs_sem.at[k],
            recv_sem=fr_sem.at[k],
            device_id=(dp, to),
            device_id_type=MESH,
        )

    def backward(k):
        to = lax.rem(ex - offset_of(k) + N, N)
        return pltpu.make_async_remote_copy(
            src_ref=ret.at[k],
            dst_ref=back.at[ex],
            send_sem=bs_sem.at[k],
            recv_sem=br_sem.at[k],
            device_id=(dp, to),
            device_id_type=MESH,
        )

    def partial(s):
        to = lax.rem(dp + s, N)
        return pltpu.make_async_remote_copy(
            src_ref=part.at[to],
            dst_ref=part_in.at[s - 1],
            send_sem=ps_sem.at[s - 1],
            recv_sem=pr_sem.at[s - 1],
            device_id=(to, ex),
            device_id_type=MESH,
        )

    @pl.loop(0, N - 1)
    def _(k):
        forward(k).start()

    recv[N - 1] = send[ex]

    for tau in range(5):
        for g in range(4):
            key = tile_key(r_col, rank_col, tau, g)
            pick_m[tau, g * TOK : (g + 1) * TOK, :] = ones_where(lane_id == key)
    small = SUB * TILE
    w_row = lax.broadcasted_iota(I32, (RB, small), 0)
    w_lane = lax.broadcasted_iota(I32, (small, RB), 1)
    c_lane = lax.broadcasted_iota(I32, (RB, small), 1)
    c_row = lax.broadcasted_iota(I32, (small, RB), 0)
    for tau in range(5):
        for g in range(4):
            owner = (w_row * 52) >> 8
            key = tile_key(owner, w_row - CAP * owner, tau, g)
            unpack_m[tau, g * RB : (g + 1) * RB, :] = ones_where(
                (c_lane == key) & (w_row < SUB * CAP)
            )
            owner = (w_lane * 52) >> 8
            key = tile_key(owner, w_lane - CAP * owner, tau, g)
            repack_m[tau, :, g * RB : (g + 1) * RB] = ones_where(
                (c_row == key) & (w_lane < SUB * CAP)
            )
    up_copy.wait()
    down_copy.wait()

    lane_small = lax.broadcasted_iota(I32, (RB, LANE), 1)

    @pl.loop(0, BATCHES)
    def _(b):
        for i in range(SUB):
            k = b * SUB + i

            @pl.when(k < N - 1)
            def _():
                forward(k).wait_recv()

        @pl.when(b == BATCHES - 1)
        def _():
            @pl.loop(0, (BATCHES - 1) * SUB)
            def _(k):
                backward(k).start()

        here = pl.ds(pl.multiple_of(b * SUB, SUB), SUB)
        rows = pl.ds(pl.multiple_of(b * RB, RB), RB)
        carry = None
        for t in range(FWD_TILES):
            tile = recv[here, t * TILE : (t + 1) * TILE, :].reshape(small, LANE)
            got = jnp.dot(unpack_m[t % 5], tile, preferred_element_type=F32)
            for g in range(4):
                group = first_group(t) + g
                piece = got[g * RB : (g + 1) * RB]
                if g == 0 and t % 5 > 0:
                    piece = piece + carry
                if g == 3 and t % 5 < 4 and t < FWD_TILES - 1:
                    carry = piece
                    continue
                if group < CHUNKS:
                    xs[:, group * LANE : (group + 1) * LANE] = piece.astype(BF)
                elif group < 2 * CHUNKS:
                    at = (group - CHUNKS) * LANE
                    sc[rows, at : at + LANE] = piece.astype(BF)
        pre = jnp.dot(xs[...], up_ref[...], preferred_element_type=F32)
        back_g = lax.dot_general(
            sc[rows, :], dn_ref[...], (((1,), (1,)), ((), ())), preferred_element_type=F32
        )
        sig = 1.0 / (1.0 + jnp.exp(-pre))
        hidden = (pre * sig).astype(BF).astype(F32)
        hid[rows, :] = hidden
        term = jnp.sum(hidden * back_g, axis=1, keepdims=True)
        high = term.astype(BF).astype(F32)
        term_tile = jnp.where(lane_small < LANE // 2, high, term - high).astype(BF)
        pre_grad = (back_g * sig * (1.0 + pre * (1.0 - sig))).astype(BF)
        row_grad = lax.dot_general(
            pre_grad, up_ref[...], (((1,), (1,)), ((), ())), preferred_element_type=F32
        ).astype(BF)
        xs[...] = row_grad
        blank = jnp.zeros((RB, LANE), BF)
        for t in range(RET_TILES):
            pieces = []
            for g in range(4):
                group = first_group(t) + g
                if group < CHUNKS:
                    pieces.append(xs[:, group * LANE : (group + 1) * LANE])
                elif group == CHUNKS:
                    pieces.append(term_tile)
                else:
                    pieces.append(blank)
            got = jnp.dot(
                repack_m[t % 5], jnp.concatenate(pieces, axis=0), preferred_element_type=F32
            )
            ret[here, t * TILE : (t + 1) * TILE, :] = got.astype(BF).reshape(SUB, TILE, LANE)

    @pl.loop((BATCHES - 1) * SUB, N - 1)
    def _(k):
        backward(k).start()

    back[ex] = ret[N - 1]

    hid_t = hid[...].T.astype(BF)
    step = 256
    for n in range(HALF // step):
        left = jnp.dot(hid_t, sc[:, n * step : (n + 1) * step], preferred_element_type=F32)
        right = jnp.dot(
            hid_t, sc[:, HALF + n * step : HALF + (n + 1) * step], preferred_element_type=F32
        )
        both = jnp.concatenate(
            [left.reshape(N, OUT_ROWS, step), right.reshape(N, OUT_ROWS, step)], axis=1
        )
        part[:, :, n * step : (n + 1) * step] = both.astype(BF)

    @pl.loop(1, N)
    def _(s):
        partial(s).start()

    @pl.loop(0, N - 1)
    def _(k):
        backward(k).wait_recv()

    carry = None
    for t in range(RET_TILES):
        tile = back[:, t * TILE : (t + 1) * TILE, :].reshape(big, LANE)
        got = jnp.dot(pick_m[t % 5], tile, preferred_element_type=F32)
        for g in range(4):
            group = first_group(t) + g
            piece = got[g * TOK : (g + 1) * TOK]
            if g == 0 and t % 5 > 0:
                piece = piece + carry
            if g == 3 and t % 5 < 4 and t < RET_TILES - 1:
                carry = piece
                continue
            if group < CHUNKS:
                token_ref[:, group * LANE : (group + 1) * LANE] = piece.astype(BF)
            elif group == CHUNKS:
                total = piece[:, 0:1] + piece[:, LANE // 2 : LANE // 2 + 1]
                gate_out_ref[...] = (total / gate).astype(BF)

    @pl.loop(1, N)
    def _(s):
        partial(s).wait_recv()

    for n in range(HALF // step):
        cols = slice(n * step, (n + 1) * step)
        total = lax.fori_loop(
            0,
            N - 1,
            lambda s, acc: acc + part_in[s, :, cols].astype(F32),
            part[dp, :, cols].astype(F32),
        )
        down_ref[:, n * step : (n + 1) * step] = total[:OUT_ROWS]
        down_ref[:, HALF + n * step : HALF + (n + 1) * step] = total[OUT_ROWS:]

    @pl.loop(0, N - 1)
    def _(k):
        forward(k).wait_send()
        backward(k).wait_send()

    @pl.loop(1, N)
    def _(s):
        partial(s).wait_send()


def body(token_values, token_scales, out_grad, route_expert, gate, up_weight, down_weight):
    vmem = pl.BlockSpec(memory_space=pltpu.VMEM)
    hbm = pl.BlockSpec(memory_space=pl.ANY)
    dma = pltpu.SemaphoreType.DMA
    token_grad, gate_grad, down_grad = pl.pallas_call(
        kernel,
        out_shape=(
            jax.ShapeDtypeStruct((TOK, D), BF),
            jax.ShapeDtypeStruct((TOK, 1), BF),
            jax.ShapeDtypeStruct((OUT_ROWS, D), F32),
        ),
        in_specs=[vmem] * 5 + [hbm] * 2,
        out_specs=(vmem, vmem, vmem),
        scratch_shapes=[
            pltpu.VMEM((D, H), BF),
            pltpu.VMEM((H, D), BF),
            pltpu.VMEM(((2 * CHUNKS + 2) * TOK, LANE), BF),
            pltpu.VMEM((N, FWD_TILES * TILE, LANE), BF),
            pltpu.VMEM((N, FWD_TILES * TILE, LANE), BF),
            pltpu.VMEM((N, RET_TILES * TILE, LANE), BF),
            pltpu.VMEM((N, RET_TILES * TILE, LANE), BF),
            pltpu.VMEM((N, 2 * OUT_ROWS, HALF), BF),
            pltpu.VMEM((N - 1, 2 * OUT_ROWS, HALF), BF),
            pltpu.VMEM((5, N * TILE, 4 * TOK), BF),
            pltpu.VMEM((5, 4 * TOK, N * TILE), BF),
            pltpu.VMEM((5, 4 * RB, SUB * TILE), BF),
            pltpu.VMEM((5, SUB * TILE, 4 * RB), BF),
            pltpu.VMEM((RB, D), BF),
            pltpu.VMEM((BATCHES * RB, H), F32),
            pltpu.VMEM((BATCHES * RB, D), BF),
            dma((2,)),
            dma((N - 1,)),
            dma((N - 1,)),
            dma((N - 1,)),
            dma((N - 1,)),
            dma((N - 1,)),
            dma((N - 1,)),
        ],
        compiler_params=pltpu.CompilerParams(
            collective_id=0, has_side_effects=True, vmem_limit_bytes=52 * 2**20
        ),
    )(token_values, token_scales, out_grad, route_expert, gate, up_weight, down_weight)
    return token_grad, gate_grad, down_grad[None]


def solution(mesh):
    return jax.shard_map(
        body,
        mesh=mesh,
        in_specs=(
            P(("dp", "expert"), None),
            P(("dp", "expert"), None),
            P(("dp", "expert"), None),
            P(("dp", "expert"), None),
            P(("dp", "expert"), None),
            P("expert", None, None),
            P("expert", None, None),
        ),
        out_specs=(P(("dp", "expert"), None), P(("dp", "expert"), None), P("expert", "dp", None)),
        check_vma=False,
    )
```

```python
import jax
import jax.numpy as jnp
from jax import lax
from jax.experimental import pallas as pl
from jax.experimental.pallas import tpu as pltpu
from jax.sharding import PartitionSpec as P

MESH = pl.DeviceIdType.MESH
BF = jnp.bfloat16
F32 = jnp.float32
I32 = jnp.int32

N = 32
TOK = 128
D = 2560
H = 768
CAP = 5
LANE = 128
CHUNKS = D // LANE
TILE = 16
FWD_TILES = 13
RET_TILES = 7
FIRST = (0, 3, 6, 9, 12)
SUB = 8
BATCHES = N // SUB
RB = 64
HALF = D // 2
OUT_ROWS = H // N
CHIPS = 16
MSG = 2 * OUT_ROWS
RELEASE = 2


def offset_of(k):
    half = (k + 1) // 2
    return jnp.where(k % 2 == 1, 16 - half, 16 + half)


def first_group(tile):
    return 16 * (tile // 5) + FIRST[tile % 5]


def tile_key(owner, rank, tau, g):
    place = rank + (CAP * (FIRST[tau] + g) - TILE * tau)
    good = (place >= 0) & (place < TILE)
    return jnp.where(good, owner * TILE + place, -1)


def ones_where(mask):
    return jnp.where(mask, 1.0, 0.0).astype(BF)


def kernel(
    values_ref, scales_ref, grad_ref, route_ref, gate_ref, up_hbm, down_hbm,
    token_ref, gate_out_ref, down_ref,
    up_ref, dn_ref, stack, send, recv, ret, back, part, pair_in, pair_sum, part_in, pack_m, pick_m, unpack_m, repack_m,
    xs, hid, sc, square,
    w_sem, fs_sem, fr_sem, bs_sem, br_sem, ps_sem, pr_sem, pair_s, pair_r,
):
    dp = lax.axis_index("dp")
    ex = lax.axis_index("expert")
    chip = dp // 2
    core = dp % 2

    up_copy = pltpu.make_async_copy(up_hbm.at[0], up_ref, w_sem.at[0])
    down_copy = pltpu.make_async_copy(down_hbm.at[0], dn_ref, w_sem.at[1])
    up_copy.start()
    down_copy.start()

    barrier = pltpu.get_barrier_semaphore()

    @pl.loop(1, N)
    def _(s):
        pl.semaphore_signal(
            barrier, inc=1, device_id=(dp, lax.rem(ex + s, N)), device_id_type=MESH
        )
        pl.semaphore_signal(
            barrier, inc=1, device_id=(lax.rem(dp + s, N), ex), device_id_type=MESH
        )

    tall = jnp.broadcast_to(route_ref[...].astype(F32), (TOK, TOK))
    wide = tall.T
    rows_i = lax.broadcasted_iota(I32, (TOK, TOK), 0)
    cols_i = lax.broadcasted_iota(I32, (TOK, TOK), 1)
    same = wide == tall
    rank_row = jnp.sum(jnp.where(same & (rows_i < cols_i), 1.0, 0.0), axis=0, keepdims=True).astype(I32)
    rank_col = jnp.sum(jnp.where(same & (cols_i < rows_i), 1.0, 0.0), axis=1, keepdims=True).astype(I32)
    r_row = route_ref[...]
    r_col = wide[:, 0:1].astype(I32)
    d_row = lax.rem(r_row - ex + N, N)

    gate = jnp.broadcast_to(gate_ref[...].astype(F32), (TOK, TOK)).T[:, 0:1]
    square[...] = jnp.zeros_like(square)
    square[0:CHUNKS, :] = scales_ref[...]
    scales = square[...].T
    for c in range(CHUNKS):
        cols = slice(c * LANE, (c + 1) * LANE)
        stack[c * TOK : (c + 1) * TOK, :] = (
            values_ref[:, cols].astype(F32) * scales[:, c : c + 1]
        ).astype(BF)
        stack[(CHUNKS + c) * TOK : (CHUNKS + c + 1) * TOK, :] = (
            gate * grad_ref[:, cols].astype(F32)
        ).astype(BF)
    stack[2 * CHUNKS * TOK :, :] = jnp.zeros((2 * TOK, LANE), BF)

    def forward(k):
        to = lax.rem(ex + offset_of(k), N)
        return pltpu.make_async_remote_copy(
            src_ref=send.at[offset_of(k)],
            dst_ref=recv.at[k],
            send_sem=fs_sem.at[k],
            recv_sem=fr_sem.at[k],
            device_id=(dp, to),
            device_id_type=MESH,
        )

    def backward(k):
        to = lax.rem(ex - offset_of(k) + N, N)
        return pltpu.make_async_remote_copy(
            src_ref=ret.at[k],
            dst_ref=back.at[ex],
            send_sem=bs_sem.at[k],
            recv_sem=br_sem.at[k],
            device_id=(dp, to),
            device_id_type=MESH,
        )

    pair_copy = pltpu.make_async_remote_copy(
        src_ref=part.at[1 - core],
        dst_ref=pair_in,
        send_sem=pair_s.at[0],
        recv_sem=pair_r.at[0],
        device_id=(2 * chip + 1 - core, ex),
        device_id_type=MESH,
    )

    def partial(s):
        to = lax.rem(chip + s, CHIPS)
        return pltpu.make_async_remote_copy(
            src_ref=pair_sum.at[to],
            dst_ref=part_in.at[s - 1],
            send_sem=ps_sem.at[s - 1],
            recv_sem=pr_sem.at[s - 1],
            device_id=(2 * to + core, ex),
            device_id_type=MESH,
        )

    big = N * TILE
    lane_id = lax.broadcasted_iota(I32, (TOK, big), 1)

    def pack(low, high):
        rows = slice(low * TILE, high * TILE)
        count = high - low
        row_id = lax.broadcasted_iota(I32, (count * TILE, TOK), 0) + low * TILE
        for tau in range(5):
            for g in range(4):
                key = tile_key(d_row, rank_row, tau, g)
                pack_m[tau, rows, g * TOK : (g + 1) * TOK] = ones_where(row_id == key)
        for t in range(FWD_TILES):
            first = first_group(t)
            got = jnp.dot(
                pack_m[t % 5, rows, :],
                stack[first * TOK : (first + 4) * TOK, :],
                preferred_element_type=F32,
            )
            send[low:high, t * TILE : (t + 1) * TILE, :] = got.astype(BF).reshape(count, TILE, LANE)

    pack(8, 24)
    pl.semaphore_wait(barrier, 2 * (N - 1))

    @pl.loop(0, N // 2)
    def _(k):
        forward(k).start()

    pack(0, 8)
    pack(24, N)

    @pl.loop(N // 2, N - 1)
    def _(k):
        forward(k).start()

    recv[N - 1] = send[0]

    for tau in range(5):
        for g in range(4):
            key = tile_key(r_col, rank_col, tau, g)
            pick_m[tau, g * TOK : (g + 1) * TOK, :] = ones_where(lane_id == key)
    small = SUB * TILE
    w_row = lax.broadcasted_iota(I32, (RB, small), 0)
    w_lane = lax.broadcasted_iota(I32, (small, RB), 1)
    c_lane = lax.broadcasted_iota(I32, (RB, small), 1)
    c_row = lax.broadcasted_iota(I32, (small, RB), 0)
    for tau in range(5):
        for g in range(4):
            owner = (w_row * 52) >> 8
            key = tile_key(owner, w_row - CAP * owner, tau, g)
            unpack_m[tau, g * RB : (g + 1) * RB, :] = ones_where(
                (c_lane == key) & (w_row < SUB * CAP)
            )
            owner = (w_lane * 52) >> 8
            key = tile_key(owner, w_lane - CAP * owner, tau, g)
            repack_m[tau, :, g * RB : (g + 1) * RB] = ones_where(
                (c_row == key) & (w_lane < SUB * CAP)
            )
    up_copy.wait()
    down_copy.wait()

    lane_small = lax.broadcasted_iota(I32, (RB, LANE), 1)

    @pl.loop(0, BATCHES)
    def _(b):
        for i in range(SUB):
            k = b * SUB + i

            @pl.when(k < N - 1)
            def _():
                forward(k).wait_recv()

        @pl.when(b == RELEASE)
        def _():
            @pl.loop(0, RELEASE * SUB)
            def _(k):
                backward(k).start()

        here = pl.ds(pl.multiple_of(b * SUB, SUB), SUB)
        rows = pl.ds(pl.multiple_of(b * RB, RB), RB)
        carry = None
        for t in range(FWD_TILES):
            tile = recv[here, t * TILE : (t + 1) * TILE, :].reshape(small, LANE)
            got = jnp.dot(unpack_m[t % 5], tile, preferred_element_type=F32)
            for g in range(4):
                group = first_group(t) + g
                piece = got[g * RB : (g + 1) * RB]
                if g == 0 and t % 5 > 0:
                    piece = piece + carry
                if g == 3 and t % 5 < 4 and t < FWD_TILES - 1:
                    carry = piece
                    continue
                if group < CHUNKS:
                    xs[:, group * LANE : (group + 1) * LANE] = piece.astype(BF)
                elif group < 2 * CHUNKS:
                    at = (group - CHUNKS) * LANE
                    sc[rows, at : at + LANE] = piece.astype(BF)
        pre = jnp.dot(xs[...], up_ref[...], preferred_element_type=F32)
        back_g = lax.dot_general(
            sc[rows, :], dn_ref[...], (((1,), (1,)), ((), ())), preferred_element_type=F32
        )
        sig = 1.0 / (1.0 + jnp.exp(-pre))
        hidden = (pre * sig).astype(BF).astype(F32)
        hid[rows, :] = hidden
        term = jnp.sum(hidden * back_g, axis=1, keepdims=True)
        high = term.astype(BF).astype(F32)
        term_tile = jnp.where(lane_small < LANE // 2, high, term - high).astype(BF)
        pre_grad = (back_g * sig * (1.0 + pre * (1.0 - sig))).astype(BF)
        row_grad = lax.dot_general(
            pre_grad, up_ref[...], (((1,), (1,)), ((), ())), preferred_element_type=F32
        ).astype(BF)
        xs[...] = row_grad
        blank = jnp.zeros((RB, LANE), BF)
        for t in range(RET_TILES):
            pieces = []
            for g in range(4):
                group = first_group(t) + g
                if group < CHUNKS:
                    pieces.append(xs[:, group * LANE : (group + 1) * LANE])
                elif group == CHUNKS:
                    pieces.append(term_tile)
                else:
                    pieces.append(blank)
            got = jnp.dot(
                repack_m[t % 5], jnp.concatenate(pieces, axis=0), preferred_element_type=F32
            )
            ret[here, t * TILE : (t + 1) * TILE, :] = got.astype(BF).reshape(SUB, TILE, LANE)

        @pl.when(b >= RELEASE)
        def _():
            @pl.loop(0, SUB)
            def _(i):
                @pl.when(b * SUB + i < N - 1)
                def _():
                    backward(b * SUB + i).start()

    back[ex] = ret[N - 1]

    hid_t = hid[...].T.astype(BF)
    step = 256
    for n in range(HALF // step):
        left = jnp.dot(hid_t, sc[:, n * step : (n + 1) * step], preferred_element_type=F32)
        right = jnp.dot(
            hid_t, sc[:, HALF + n * step : HALF + (n + 1) * step], preferred_element_type=F32
        )
        both = jnp.concatenate(
            [left.reshape(N, OUT_ROWS, step), right.reshape(N, OUT_ROWS, step)], axis=1
        ).astype(BF)
        both = both.reshape(CHIPS, 2, MSG, step)
        for c in range(2):
            part[c, :, :, n * step : (n + 1) * step] = both[:, c]

    pair_copy.start()
    pair_copy.wait_recv()

    @pl.loop(1, CHIPS + 1)
    def _(s):
        to = lax.rem(chip + s, CHIPS)
        pair_sum[to] = (part[core, to].astype(F32) + pair_in[to].astype(F32)).astype(BF)

        @pl.when(s < CHIPS)
        def _():
            partial(s).start()

    @pl.loop(1, CHIPS)
    def _(s):
        partial(s).wait_recv()

    for n in range(HALF // step):
        cols = slice(n * step, (n + 1) * step)
        total = lax.fori_loop(
            0,
            CHIPS - 1,
            lambda s, acc: acc + part_in[s, :, cols].astype(F32),
            pair_sum[chip, :, cols].astype(F32),
        )
        down_ref[:, n * step : (n + 1) * step] = total[:OUT_ROWS]
        down_ref[:, HALF + n * step : HALF + (n + 1) * step] = total[OUT_ROWS:]

    @pl.loop(0, N - 1)
    def _(k):
        forward(k).wait_send()

    @pl.loop(1, CHIPS)
    def _(s):
        partial(s).wait_send()

    pair_copy.wait_send()

    @pl.loop(0, N - 1)
    def _(k):
        backward(k).wait_send()
        backward(k).wait_recv()

    carry = None
    for t in range(RET_TILES):
        tile = back[:, t * TILE : (t + 1) * TILE, :].reshape(big, LANE)
        got = jnp.dot(pick_m[t % 5], tile, preferred_element_type=F32)
        for g in range(4):
            group = first_group(t) + g
            piece = got[g * TOK : (g + 1) * TOK]
            if g == 0 and t % 5 > 0:
                piece = piece + carry
            if g == 3 and t % 5 < 4 and t < RET_TILES - 1:
                carry = piece
                continue
            if group < CHUNKS:
                token_ref[:, group * LANE : (group + 1) * LANE] = piece.astype(BF)
            elif group == CHUNKS:
                total = piece[:, 0:1] + piece[:, LANE // 2 : LANE // 2 + 1]
                gate_out_ref[...] = (total / gate).astype(BF)


def body(token_values, token_scales, out_grad, route_expert, gate, up_weight, down_weight):
    vmem = pl.BlockSpec(memory_space=pltpu.VMEM)
    hbm = pl.BlockSpec(memory_space=pl.ANY)
    dma = pltpu.SemaphoreType.DMA
    token_grad, gate_grad, down_grad = pl.pallas_call(
        kernel,
        out_shape=(
            jax.ShapeDtypeStruct((TOK, D), BF),
            jax.ShapeDtypeStruct((TOK, 1), BF),
            jax.ShapeDtypeStruct((OUT_ROWS, D), F32),
        ),
        in_specs=[vmem] * 5 + [hbm] * 2,
        out_specs=(vmem, vmem, vmem),
        scratch_shapes=[
            pltpu.VMEM((D, H), BF),
            pltpu.VMEM((H, D), BF),
            pltpu.VMEM(((2 * CHUNKS + 2) * TOK, LANE), BF),
            pltpu.VMEM((N, FWD_TILES * TILE, LANE), BF),
            pltpu.VMEM((N, FWD_TILES * TILE, LANE), BF),
            pltpu.VMEM((N, RET_TILES * TILE, LANE), BF),
            pltpu.VMEM((N, RET_TILES * TILE, LANE), BF),
            pltpu.VMEM((2, CHIPS, MSG, HALF), BF),
            pltpu.VMEM((CHIPS, MSG, HALF), BF),
            pltpu.VMEM((CHIPS, MSG, HALF), BF),
            pltpu.VMEM((CHIPS - 1, MSG, HALF), BF),
            pltpu.VMEM((5, N * TILE, 4 * TOK), BF),
            pltpu.VMEM((5, 4 * TOK, N * TILE), BF),
            pltpu.VMEM((5, 4 * RB, SUB * TILE), BF),
            pltpu.VMEM((5, SUB * TILE, 4 * RB), BF),
            pltpu.VMEM((RB, D), BF),
            pltpu.VMEM((BATCHES * RB, H), F32),
            pltpu.VMEM((BATCHES * RB, D), BF),
            pltpu.VMEM((TOK, TOK), F32),
            dma((2,)),
            dma((N - 1,)),
            dma((N - 1,)),
            dma((N - 1,)),
            dma((N - 1,)),
            dma((CHIPS - 1,)),
            dma((CHIPS - 1,)),
            dma((1,)),
            dma((1,)),
        ],
        compiler_params=pltpu.CompilerParams(
            collective_id=0, has_side_effects=True, vmem_limit_bytes=52 * 2**20
        ),
    )(
        token_values,
        token_scales.T,
        out_grad,
        route_expert.reshape(1, TOK),
        gate.reshape(1, TOK),
        up_weight,
        down_weight,
    )
    return token_grad, gate_grad, down_grad[None]


def solution(mesh):
    return jax.shard_map(
        body,
        mesh=mesh,
        in_specs=(
            P(("dp", "expert"), None),
            P(("dp", "expert"), None),
            P(("dp", "expert"), None),
            P(("dp", "expert"), None),
            P(("dp", "expert"), None),
            P("expert", None, None),
            P("expert", None, None),
        ),
        out_specs=(P(("dp", "expert"), None), P(("dp", "expert"), None), P("expert", "dp", None)),
        check_vma=False,
    )
```
